1024 devices in a mesh: dp: 64 (over z, y_hi, core), seq: 16 (over y_lo, x).
Axes of the slice: x: 8, y: 8 (y_hi: 4, y_lo: 2; y = y_hi * 2 + y_lo), z: 8, core: 2. Of those that a mesh axis runs over, the one named last changes fastest.
Arguments:
- enc_final: bfloat16 [64, 384, 4096], P('dp', 'seq'), may hold values from -6 to 6
- norm_gain: float32 [4096], replicated, may hold values from 0.1 to 1.9
- dec_queries: bfloat16 [2, 64, 2048, 2048], P(None, 'dp', 'seq'), may hold values from -48 to 48
- out_grad: bfloat16 [2, 64, 2048, 2048], P(None, 'dp', 'seq'), may hold values from -6 to 6
- enc_keys: bfloat16 [2, 64, 384, 2048], P(None, 'dp', 'seq'), may hold values from -6 to 6
- enc_values: bfloat16 [2, 64, 384, 2048], P(None, 'dp', 'seq'), may hold values from -6 to 6
- key_weight: bfloat16 [2, 4096, 2048], P(None, None, 'seq'), may hold values from -0.09375 to 0.09375
- value_weight: bfloat16 [2, 4096, 2048], P(None, None, 'seq'), may hold values from -0.09375 to 0.09375
Outputs:
- enc_grad: bfloat16 [64, 384, 4096], P('dp', 'seq')
- gain_grad: float32 [4096], replicated
The draws below stay inside these ranges and needn't reach their ends.
All inputs are finite; a program needn't handle non-finite values.
Results may differ from the reference program's by a relative error of at most 0.007.
Values may be sent and summed in bfloat16 or wider, within the bound.
A program may use at most 128 MiB of HBM per device.

```python
import jax
import jax.numpy as jnp
from jax import lax

D = 4096
HEADS = 32
HEAD_DIM = 64
LAYERS = 2
HD = 2048
DOCS = 64
ENC = 384
DEC = 2048


def shared_keys(key):
    base = jax.random.normal(jax.random.fold_in(key, 101), (LAYERS, DOCS, ENC, HD), jnp.float32)
    return jnp.clip(base, -6.0, 6.0)


def draw_enc_keys(key, part):
    return shared_keys(key).astype(jnp.bfloat16)


def draw_dec_queries(key, part):
    drawn = 0.125 * jax.random.normal(jax.random.fold_in(key, 103), (LAYERS, DOCS, DEC, HD), jnp.float32)
    drawn = jnp.clip(drawn, -0.75, 0.75)
    return drawn.astype(jnp.bfloat16)


def level_of(stream_key, extent, split, smallest, largest):
    def one(position, blocks):
        draws = jax.random.uniform(jax.random.fold_in(jax.random.fold_in(stream_key, 6), position), (blocks,), jnp.float32, smallest / len(split), largest / len(split))
        return jnp.repeat(jnp.exp(draws), extent[position] // blocks).reshape((-1,) + (1,) * (len(extent) - position - 1))

    factor_of = one(*split[0])
    for cut in split[1:]:
        factor_of = factor_of * one(*cut)
    return factor_of


def normal_values(stream_key, shape, spread, reach, pieces=(), dtype=jnp.bfloat16):
    values = spread * jax.random.normal(stream_key, shape, jnp.float32)
    if pieces:
        values = values * level_of(stream_key, shape, pieces, -0.22, 0.18)
    return jnp.clip(values, -reach, reach).astype(dtype)


def setup_inputs(seed: int = 0) -> dict:
    key_list = jax.random.split(jax.random.key(seed), 9)
    return {
        "enc_final": normal_values(key_list[0], (DOCS, ENC, D), 1.0, 6.0, ((0, 64), (1, 16))),
        "norm_gain": jnp.clip(1.0 + 0.18 * jax.random.normal(key_list[1], (D,), jnp.float32), 0.1, 1.9),
        "dec_queries": draw_dec_queries(jax.random.fold_in(key_list[8], 71), 0),
        "out_grad": normal_values(key_list[3], (LAYERS, DOCS, DEC, HD), 1.0, 6.0, ((1, 64), (2, 16))),
        "enc_keys": draw_enc_keys(jax.random.fold_in(key_list[8], 71), 0),
        "enc_values": normal_values(key_list[5], (LAYERS, DOCS, ENC, HD), 1.0, 6.0, ((1, 64), (2, 16))),
        "key_weight": normal_values(key_list[6], (LAYERS, D, HD), D ** -0.5, 0.09375, ((2, 16),)),
        "value_weight": normal_values(key_list[7], (LAYERS, D, HD), D ** -0.5, 0.09375, ((2, 16),)),
    }


def attention_grads(query_rows, grad_rows, key_rows, value_rows):
    dec_count = query_rows.shape[0]
    enc_count = key_rows.shape[0]
    query_heads = query_rows.astype(jnp.float32).reshape(dec_count, HEADS, HEAD_DIM)
    grad_heads = grad_rows.astype(jnp.float32).reshape(dec_count, HEADS, HEAD_DIM)
    key_heads = key_rows.astype(jnp.float32).reshape(enc_count, HEADS, HEAD_DIM)
    value_heads = value_rows.astype(jnp.float32).reshape(enc_count, HEADS, HEAD_DIM)
    scores = jnp.einsum('qhd,khd->hqk', query_heads, key_heads)
    row_peak = lax.optimization_barrier(jnp.max(scores, axis=-1, keepdims=True))
    shifted = jnp.exp(scores - row_peak)
    weights = shifted / lax.optimization_barrier(jnp.sum(shifted, axis=-1, keepdims=True))
    weights_low = weights.astype(jnp.bfloat16).astype(jnp.float32)
    prob_grad = jnp.einsum('qhd,khd->hqk', grad_heads, value_heads)
    row_delta = lax.optimization_barrier(jnp.sum(weights * prob_grad, axis=-1, keepdims=True))
    score_grad = (weights * (prob_grad - row_delta)).astype(jnp.bfloat16).astype(jnp.float32)
    value_grad = jnp.einsum('hqk,qhd->khd', weights_low, grad_heads).reshape(enc_count, HEADS * HEAD_DIM)
    key_grad = jnp.einsum('hqk,qhd->khd', score_grad, query_heads).reshape(enc_count, HEADS * HEAD_DIM)
    return (key_grad.astype(jnp.bfloat16), value_grad.astype(jnp.bfloat16))

def reference(enc_final, norm_gain, dec_queries, out_grad, enc_keys, enc_values, key_weight, value_weight):

    def one_document(inputs):
        final_rows, query_all, grad_all, key_all, value_all = inputs
        state_grad = jnp.zeros((final_rows.shape[0], final_rows.shape[1]), jnp.float32)
        for layer_index in range(LAYERS):
            key_grad, value_grad = attention_grads(query_all[layer_index], grad_all[layer_index], key_all[layer_index], value_all[layer_index])
            state_grad = state_grad + jnp.dot(key_grad, key_weight[layer_index].T, preferred_element_type=jnp.float32)
            state_grad = state_grad + jnp.dot(value_grad, value_weight[layer_index].T, preferred_element_type=jnp.float32)
        final_float = final_rows.astype(jnp.float32)
        inv_rms = lax.rsqrt(lax.optimization_barrier(jnp.mean(final_float * final_float, axis=-1, keepdims=True)) + 1e-06)
        normed = final_float * inv_rms
        scaled = norm_gain[None, :] * state_grad
        grad_rows = inv_rms * (scaled - normed * lax.optimization_barrier(jnp.mean(scaled * normed, axis=-1, keepdims=True)))
        gain_term = lax.optimization_barrier(jnp.sum(state_grad * normed, axis=0))
        return (grad_rows.astype(jnp.bfloat16), gain_term)
    inputs = (enc_final, jnp.moveaxis(dec_queries, 1, 0), jnp.moveaxis(out_grad, 1, 0), jnp.moveaxis(enc_keys, 1, 0), jnp.moveaxis(enc_values, 1, 0))
    enc_grad, gain_terms = lax.map(one_document, inputs)
    gain_grad = lax.optimization_barrier(jnp.sum(gain_terms, axis=0)) / DOCS
    return (enc_grad, gain_grad)
```

```python
import functools

import jax
import jax.numpy as jnp
from jax import lax
from jax.experimental import pallas as pl
from jax.experimental.pallas import tpu as pltpu
from jax.sharding import PartitionSpec as P

MESH = pl.DeviceIdType.MESH
HEAD_DIM = 64
LANES = 128
RING = 8
ROWS = 2
SHIFTS = (0, 4, 3, 5, 2, 6, 1, 7)
CHAINS = ((1, 0, 4, 0), (-1, 1, 4, 4), (1, 1, 3, 8), (-1, 0, 3, 11))
CHAIN_SLOTS = 14

TRANSPOSED = (((1,), (1,)), ((), ()))


def kernel(
    low_count, z_count,
    enc_ref, gain_ref, q_ref, g_ref, k_ref, v_ref, kw_ref, vw_ref,
    out_ref, gout_ref,
    qb, gb, kb, vb, km, vm, acc_k, acc_v, w, g_own, g_far, part, normed, inv,
    c_send, c_recv, a_send, a_recv, b_send, b_recv, z_send, z_recv, t_recv,
    tok_s, tok_r, kv_s, kv_r, own_s, w_s, w_r, f_s, f_r, x_s, x_r, c_s, c_r,
    a_s, a_r, b_s, b_r, z_s, z_r, t_s, t_r,
):
    layers = q_ref.shape[0]
    dec = q_ref.shape[2]
    enc = k_ref.shape[2]
    enc_all = enc * RING * ROWS
    width = enc_ref.shape[1]
    half = width // 2
    piece = width // (RING * ROWS)
    yh_count = low_count // 2

    seq = lax.axis_index("seq")
    dp = lax.axis_index("dp")
    x = lax.rem(seq, RING)
    y = seq // RING
    low = lax.rem(dp, low_count)
    z = dp // low_count
    core = lax.rem(low, 2)
    y_hi = low // 2

    def member(dx, dy):
        return lax.rem(y + dy, ROWS) * RING + lax.rem(x + dx + RING, RING)

    def columns(index, size):
        return pl.ds(pl.multiple_of(index * size, size), size)

    others = [(dx, dy) for dx in SHIFTS for dy in range(ROWS) if (dx, dy) != (0, 0)]
    across = member(0, 1)
    far_yh = lax.rem(y_hi + 2 * y - 1 + yh_count, yh_count)
    far_dp = z * low_count + far_yh * 2 + core
    low_dps = [z * low_count + lax.rem(low + j, low_count) for j in range(1, low_count)]
    z_dps = [lax.rem(z + j, z_count) * low_count + low for j in range(1, z_count)]

    barrier = pltpu.get_barrier_semaphore()
    for dx, dy in others:
        pl.semaphore_signal(
            barrier, inc=1, device_id={"seq": member(dx, dy)}, device_id_type=MESH
        )
    for other in low_dps + z_dps:
        pl.semaphore_signal(barrier, inc=1, device_id={"dp": other}, device_id_type=MESH)
    pl.semaphore_signal(
        barrier, inc=1, device_id={"dp": far_dp, "seq": across}, device_id_type=MESH
    )

    own = []
    for layer in range(layers):
        for n, (src, dst) in enumerate(((q_ref, qb), (g_ref, gb))):
            own.append(
                pltpu.make_async_copy(
                    src.at[layer, 0, :, columns(seq, LANES)],
                    dst.at[layer, 0, pl.ds(0, dec)],
                    tok_r.at[layer, n, 0, 0],
                )
            )
    own_kv = []
    for n, (src, dst) in enumerate(((k_ref, kb), (v_ref, vb))):
        own_kv.append(
            pltpu.make_async_copy(
                src.at[:, 0, :, columns(seq, LANES)], dst.at[seq], kv_r.at[n, 0, 0]
            )
        )
    own_w = []
    for layer in range(layers):
        for n, src in enumerate((kw_ref, vw_ref)):
            own_w.append(
                pltpu.make_async_copy(
                    src.at[layer],
                    w.at[:, pl.ds((2 * layer + n) * LANES, LANES)],
                    own_s.at[layer, n],
                )
            )
    for copy in own_kv + own + own_w:
        copy.start()

    pl.semaphore_wait(barrier, len(others) + len(low_dps) + len(z_dps) + 1)

    kv_copies = []
    for dx, dy in others:
        to = member(dx, dy)
        for n, (src, dst) in enumerate(((k_ref, kb), (v_ref, vb))):
            kv_copies.append(
                pltpu.make_async_remote_copy(
                    src.at[:, 0, :, columns(to, LANES)],
                    dst.at[seq],
                    kv_s.at[n, dx, dy],
                    kv_r.at[n, dx, dy],
                    device_id={"seq": to},
                    device_id_type=MESH,
                )
            )
    for copy in kv_copies:
        copy.start()

    w_dp = jnp.where(core == 0, dp, far_dp)
    w_copies = []
    for n, src in enumerate((kw_ref, vw_ref)):
        w_copies.append(
            pltpu.make_async_remote_copy(
                src.at[core],
                w.at[:, columns(2 * layers + 2 * core + n, LANES)],
                w_s.at[n],
                w_r.at[n],
                device_id={"dp": w_dp, "seq": across},
                device_id_type=MESH,
            )
        )

    tok_copies = []
    for layer in range(layers):
        for slot, dx in enumerate(SHIFTS):
            for dy in range(ROWS):
                if (dx, dy) == (0, 0):
                    continue
                to = member(dx, dy)
                for n, (src, dst) in enumerate(((q_ref, qb), (g_ref, gb))):
                    copy = pltpu.make_async_remote_copy(
                        src.at[layer, 0, :, columns(to, LANES)],
                        dst.at[layer, slot, pl.ds(dy * dec, dec)],
                        tok_s.at[layer, n, slot, dy],
                        tok_r.at[layer, n, slot, dy],
                        device_id={"seq": to},
                        device_id_type=MESH,
                    )
                    copy.start()
                    tok_copies.append(copy)
            if layer == 0 and slot == 1:
                for copy in w_copies:
                    copy.start()

    final = enc_ref[...].astype(jnp.float32)
    inv[...] = lax.rsqrt(jnp.mean(final * final, axis=-1, keepdims=True) + 1e-6)
    normed[...] = final * inv[...]

    for copy in own_kv:
        copy.wait()
    for copy in kv_copies:
        copy.wait_recv()

    first_head = lax.broadcasted_iota(jnp.int32, (enc_all, LANES), 1) < HEAD_DIM
    exchanges = []
    for layer in range(layers):
        for src, dst in ((kb, km), (vb, vm)):
            rows = src[:, layer].astype(jnp.float32).reshape(enc_all, LANES)
            dst[pl.ds(0, enc_all), :] = jnp.where(first_head, rows, 0.0).astype(jnp.bfloat16)
            dst[pl.ds(enc_all, enc_all), :] = jnp.where(first_head, 0.0, rows).astype(jnp.bfloat16)
        acc_k[...] = jnp.zeros_like(acc_k)
        acc_v[...] = jnp.zeros_like(acc_v)

        def tokens(slot, carry, layer=layer):
            for n, dst in enumerate((qb, gb)):
                for dy in range(ROWS):
                    there = dst.at[layer, slot, pl.ds(dy * dec, dec)]
                    pltpu.make_async_copy(there, there, tok_r.at[layer, n, slot, dy]).wait()
            queries = qb[layer, slot]
            grads = gb[layer, slot]
            count = queries.shape[0]
            scores = lax.dot_general(
                km[...], queries, TRANSPOSED, preferred_element_type=jnp.float32
            ).reshape(2, enc_all, count)
            prob_grad = lax.dot_general(
                vm[...], grads, TRANSPOSED, preferred_element_type=jnp.float32
            ).reshape(2, enc_all, count)
            shifted = jnp.exp(scores - jnp.max(scores, axis=1, keepdims=True))
            probs = shifted * (1.0 / jnp.sum(shifted, axis=1, keepdims=True))
            delta = jnp.sum(probs * prob_grad, axis=1, keepdims=True)
            score_grad = (probs * (prob_grad - delta)).astype(jnp.bfloat16)
            acc_v[...] += jnp.dot(
                probs.astype(jnp.bfloat16).reshape(2 * enc_all, count),
                grads,
                preferred_element_type=jnp.float32,
            )
            acc_k[...] += jnp.dot(
                score_grad.reshape(2 * enc_all, count),
                queries,
                preferred_element_type=jnp.float32,
            )
            return carry

        lax.fori_loop(0, RING, tokens, 0)

        side = enc_all // ROWS
        for n, acc in enumerate((acc_k, acc_v)):
            grad = jnp.where(
                first_head, acc[pl.ds(0, enc_all), :], acc[pl.ds(enc_all, enc_all), :]
            ).astype(jnp.bfloat16)
            for row in range(ROWS):
                g_own[row, :, pl.ds((2 * layer + n) * LANES, LANES)] = grad[
                    row * side : (row + 1) * side
                ]
        block = pl.ds(2 * layer * LANES, 2 * LANES)
        exchange = pltpu.make_async_remote_copy(
            g_own.at[1 - y, :, block],
            g_far.at[:, block],
            x_s.at[layer],
            x_r.at[layer],
            device_id={"seq": across},
            device_id_type=MESH,
        )
        exchange.start()
        exchanges.append(exchange)

        if layer == 0:
            for copy in own_w:
                copy.wait()
            for copy in w_copies:
                copy.wait()
            there = w.at[:, columns(layers + core, 2 * LANES)]
            handed = pltpu.make_async_remote_copy(
                there,
                there,
                f_s,
                f_r,
                device_id={"dp": dp + 1 - 2 * core},
                device_id_type=MESH,
            )
            handed.start()

    own_depth = 2 * layers * LANES
    tile = min(512, half)

    def project(first, grads, depth_start, add):
        def one(index, carry):
            at = first + index
            weights = w[columns(at, tile), pl.ds(depth_start, own_depth)]
            terms = lax.dot_general(
                grads, weights, TRANSPOSED, preferred_element_type=jnp.float32
            ).reshape(RING, enc, tile)
            if add:
                terms = terms + part[:, :, columns(at, tile)]
            part[:, :, columns(at, tile)] = terms
            return carry

        lax.fori_loop(0, half // tile, one, 0)

    mine = g_own[y]
    project(0, mine, 0, False)
    project(half // tile, mine, 0, False)
    handed.wait()
    for exchange in exchanges:
        exchange.wait_recv()
    theirs = g_far[...]

    hops = {}

    def term(dx, side_of):
        return part[lax.rem(x + dx + RING, RING), :, pl.ds(side_of * half, half)]

    def hop(chain, k):
        way, side_of, length, first = CHAINS[chain]
        total = term(way * (length - k), side_of)
        if k:
            hops[chain, k - 1].wait_recv()
            total = total + c_recv[first + k - 1].astype(jnp.float32)
        c_send[first + k] = total.astype(jnp.bfloat16)
        copy = pltpu.make_async_remote_copy(
            c_send.at[first + k],
            c_recv.at[first + k],
            c_s.at[first + k],
            c_r.at[first + k],
            device_id={"seq": member(way, 0)},
            device_id_type=MESH,
        )
        copy.start()
        hops[chain, k] = copy

    project(0, theirs, own_depth, True)
    hop(0, 0)
    hop(3, 0)
    project(half // tile, theirs, own_depth, True)
    hop(1, 0)
    hop(2, 0)
    for copy in kv_copies + tok_copies + exchanges:
        copy.wait_send()
    for k in range(1, 4):
        hop(0, k)
        hop(1, k)
        if k < 3:
            hop(2, k)
            hop(3, k)

    arrived = []
    for side_of in range(2):
        total = term(0, side_of)
        for chain, (way, chain_side, length, first) in enumerate(CHAINS):
            if chain_side == side_of:
                hops[chain, length - 1].wait_recv()
                total = total + c_recv[first + length - 1].astype(jnp.float32)
        arrived.append(total)

    a_copies = []
    for side_of in range(2):
        state = arrived[side_of]
        cols = pl.ds(side_of * half, half)
        part[0, :, cols] = state
        gains = jnp.sum(state * normed[:, cols], axis=0, keepdims=True)
        for s in range(RING):
            a_send[side_of * RING + s] = gains[:, s * piece : (s + 1) * piece]
    for j, (dx, dy) in enumerate(others):
        to = member(dx, dy)
        copy = pltpu.make_async_remote_copy(
            a_send.at[to],
            a_recv.at[j],
            a_s.at[j],
            a_r.at[j],
            device_id={"seq": to},
            device_id_type=MESH,
        )
        copy.start()
        a_copies.append(copy)

    state = part[0]
    scaled = gain_ref[...] * state
    mean = jnp.mean(scaled * normed[...], axis=-1, keepdims=True)
    out_ref[...] = (inv[...] * (scaled - normed[...] * mean)).astype(jnp.bfloat16)

    total = a_send[seq]
    for copy in a_copies:
        copy.wait_recv()
    for j in range(len(others)):
        total = total + a_recv[j]

    def everyone(total, send, recv, here, dps, ss, rs):
        send[...] = total
        recv[here] = total
        copies = []
        for j, other in enumerate(dps):
            copy = pltpu.make_async_remote_copy(
                send,
                recv.at[here],
                ss.at[j],
                rs.at[j],
                device_id={"dp": other},
                device_id_type=MESH,
            )
            copy.start()
            copies.append(copy)
        for copy in copies:
            copy.wait_recv()
        total = recv[0]
        for j in range(1, len(dps) + 1):
            total = total + recv[j]
        return total, copies

    total, b_copies = everyone(total, b_send, b_recv, low, low_dps, b_s, b_r)
    total, z_copies = everyone(total, z_send, z_recv, z, z_dps, z_s, z_r)

    t_recv[seq] = total * (1.0 / (low_count * z_count))
    t_copies = []
    for j, (dx, dy) in enumerate(others):
        copy = pltpu.make_async_remote_copy(
            t_recv.at[seq],
            t_recv.at[seq],
            t_s.at[j],
            t_r.at[j],
            device_id={"seq": member(dx, dy)},
            device_id_type=MESH,
        )
        copy.start()
        t_copies.append(copy)
    for copy in list(hops.values()) + a_copies + b_copies + z_copies:
        copy.wait_send()
    for copy in t_copies:
        copy.wait()
    for s in range(RING * ROWS):
        gout_ref[:, pl.ds(s * piece, piece)] = t_recv[s]


def body(low_count, z_count, enc_final, norm_gain, q, g, k, v, kw, vw):
    enc, width = enc_final.shape[1:]
    layers, _, dec, _ = q.shape
    group = RING * ROWS
    enc_all = enc * group
    half = width // 2
    piece = width // group
    bf, f32 = jnp.bfloat16, jnp.float32
    dma = pltpu.SemaphoreType.DMA
    vmem = pltpu.VMEM
    outs = pl.pallas_call(
        functools.partial(kernel, low_count, z_count),
        out_shape=(
            jax.ShapeDtypeStruct((enc, width), bf),
            jax.ShapeDtypeStruct((1, width), f32),
        ),
        in_specs=[pl.BlockSpec(memory_space=vmem)] * 2 + [pl.BlockSpec(memory_space=pl.ANY)] * 6,
        out_specs=(pl.BlockSpec(memory_space=vmem),) * 2,
        scratch_shapes=[
            vmem((layers, RING, ROWS * dec, LANES), bf),
            vmem((layers, RING, ROWS * dec, LANES), bf),
            vmem((group, layers, enc, LANES), bf),
            vmem((group, layers, enc, LANES), bf),
            vmem((2 * enc_all, LANES), bf),
            vmem((2 * enc_all, LANES), bf),
            vmem((2 * enc_all, LANES), f32),
            vmem((2 * enc_all, LANES), f32),
            vmem((width, 4 * layers * LANES), bf),
            vmem((ROWS, enc_all // ROWS, 2 * layers * LANES), bf),
            vmem((enc_all // ROWS, 2 * layers * LANES), bf),
            vmem((RING, enc, width), f32),
            vmem((enc, width), f32),
            vmem((enc, 1), f32),
            vmem((CHAIN_SLOTS, enc, half), bf),
            vmem((CHAIN_SLOTS, enc, half), bf),
            vmem((group, 1, piece), f32),
            vmem((group, 1, piece), f32),
            vmem((1, piece), f32),
            vmem((low_count, 1, piece), f32),
            vmem((1, piece), f32),
            vmem((z_count, 1, piece), f32),
            vmem((group, 1, piece), f32),
            dma((layers, 2, RING, ROWS)),
            dma((layers, 2, RING, ROWS)),
            dma((2, RING, ROWS)),
            dma((2, RING, ROWS)),
            dma((layers, 2)),
            dma((2,)),
            dma((2,)),
            dma(()),
            dma(()),
            dma((layers,)),
            dma((layers,)),
            dma((CHAIN_SLOTS,)),
            dma((CHAIN_SLOTS,)),
            dma((group,)),
            dma((group,)),
            dma((low_count,)),
            dma((low_count,)),
            dma((z_count,)),
            dma((z_count,)),
            dma((group,)),
            dma((group,)),
        ],
        compiler_params=pltpu.CompilerParams(
            collective_id=0, has_side_effects=True, vmem_limit_bytes=56 * 2**20
        ),
    )(enc_final[0], norm_gain[None], q, g, k, v, kw, vw)
    return outs[0][None], outs[1][0]


def solution(mesh):
    count = mesh.shape["dp"]
    low_count = min(8, count)
    placed = (
        P("dp", "seq", None),
        P(),
        P(None, "dp", "seq", None),
        P(None, "dp", "seq", None),
        P(None, "dp", "seq", None),
        P(None, "dp", "seq", None),
        P(None, None, "seq"),
        P(None, None, "seq"),
    )
    return jax.shard_map(
        functools.partial(body, low_count, count // low_count),
        mesh=mesh,
        in_specs=placed,
        out_specs=(P("dp", "seq", None), P()),
        check_vma=False,
    )
```

```python
import functools

import jax
import jax.numpy as jnp
from jax import lax
from jax.experimental import pallas as pl
from jax.experimental.pallas import tpu as pltpu
from jax.sharding import PartitionSpec as P

MESH = pl.DeviceIdType.MESH
HEAD_DIM = 64
LANES = 128
RING = 8
ROWS = 2
SHIFTS = (0, 4, 3, 5, 2, 6, 1, 7)
PARTS = (0, 2, 1, 3)
HOPS = ((4, 3), (4, 3), (3, 4), (3, 4))
FIRST = tuple(tuple(sum(h[0] + h[1] for h in HOPS[:p]) + d * HOPS[p][0] for d in (0, 1)) for p in range(4))
CHAIN_SLOTS = sum(h[0] + h[1] for h in HOPS)

TRANSPOSED = (((1,), (1,)), ((), ()))


def kernel(
    low_count, z_count,
    enc_ref, gain_ref, q_ref, g_ref, k_ref, v_ref, kw_ref, vw_ref,
    out_ref, gout_ref,
    qb, gb, kb, vb, km, vm, acc_k, acc_v, w, g_own, g_far, part, final_state, normed, inv,
    c_send, c_recv, a_send, a_recv, b_send, b_recv, z_send, z_recv, t_recv,
    tok_s, tok_r, kv_s, kv_r, own_s, w_s, w_r, f_s, f_r, x_s, x_r, c_s, c_r,
    a_s, a_r, b_s, b_r, z_s, z_r, t_s, t_r,
):
    layers = q_ref.shape[0]
    dec = q_ref.shape[2]
    enc = k_ref.shape[2]
    enc_all = enc * RING * ROWS
    width = enc_ref.shape[1]
    quarter = width // 4
    piece = width // (RING * ROWS)
    yh_count = low_count // 2

    seq = lax.axis_index("seq")
    dp = lax.axis_index("dp")
    x = lax.rem(seq, RING)
    y = seq // RING
    low = lax.rem(dp, low_count)
    z = dp // low_count
    core = lax.rem(low, 2)
    y_hi = low // 2

    def member(dx, dy):
        return lax.rem(y + dy, ROWS) * RING + lax.rem(x + dx + RING, RING)

    def columns(index, size):
        return pl.ds(pl.multiple_of(index * size, size), size)

    others = [(dx, dy) for dx in SHIFTS for dy in range(ROWS) if (dx, dy) != (0, 0)]
    across = member(0, 1)
    far_yh = lax.rem(y_hi + 2 * y - 1 + yh_count, yh_count)
    far_dp = z * low_count + far_yh * 2 + core
    low_dps = [z * low_count + lax.rem(low + j, low_count) for j in range(1, low_count)]
    z_dps = [lax.rem(z + j, z_count) * low_count + low for j in range(1, z_count)]

    barrier = pltpu.get_barrier_semaphore()
    for dx, dy in others:
        pl.semaphore_signal(
            barrier, inc=1, device_id={"seq": member(dx, dy)}, device_id_type=MESH
        )
    for other in low_dps + z_dps:
        pl.semaphore_signal(barrier, inc=1, device_id={"dp": other}, device_id_type=MESH)
    pl.semaphore_signal(
        barrier, inc=1, device_id={"dp": far_dp, "seq": across}, device_id_type=MESH
    )

    own = []
    for layer in range(layers):
        for n, (src, dst) in enumerate(((q_ref, qb), (g_ref, gb))):
            own.append(
                pltpu.make_async_copy(
                    src.at[layer, 0, :, columns(seq, LANES)],
                    dst.at[layer, 0, pl.ds(0, dec)],
                    tok_r.at[layer, n, 0, 0],
                )
            )
    own_kv = []
    for n, (src, dst) in enumerate(((k_ref, kb), (v_ref, vb))):
        own_kv.append(
            pltpu.make_async_copy(
                src.at[:, 0, :, columns(seq, LANES)], dst.at[seq], kv_r.at[n, 0, 0]
            )
        )
    own_w = []
    for layer in range(layers):
        for n, src in enumerate((kw_ref, vw_ref)):
            own_w.append(
                pltpu.make_async_copy(
                    src.at[layer],
                    w.at[:, pl.ds((2 * layer + n) * LANES, LANES)],
                    own_s.at[layer, n],
                )
            )
    for copy in own_kv + own:
        copy.start()

    pl.semaphore_wait(barrier, len(others) + len(low_dps) + len(z_dps) + 1)

    kv_copies = []
    for dx, dy in others:
        to = member(dx, dy)
        for n, (src, dst) in enumerate(((k_ref, kb), (v_ref, vb))):
            kv_copies.append(
                pltpu.make_async_remote_copy(
                    src.at[:, 0, :, columns(to, LANES)],
                    dst.at[seq],
                    kv_s.at[n, dx, dy],
                    kv_r.at[n, dx, dy],
                    device_id={"seq": to},
                    device_id_type=MESH,
                )
            )
    for copy in kv_copies:
        copy.start()

    w_dp = jnp.where(core == 0, dp, far_dp)
    w_copies = []
    for n, src in enumerate((kw_ref, vw_ref)):
        w_copies.append(
            pltpu.make_async_remote_copy(
                src.at[core],
                w.at[:, columns(2 * layers + 2 * core + n, LANES)],
                w_s.at[n],
                w_r.at[n],
                device_id={"dp": w_dp, "seq": across},
                device_id_type=MESH,
            )
        )

    tok_copies = []
    for layer in range(layers):
        for slot, dx in enumerate(SHIFTS):
            for dy in range(ROWS):
                if (dx, dy) == (0, 0):
                    continue
                to = member(dx, dy)
                for n, (src, dst) in enumerate(((q_ref, qb), (g_ref, gb))):
                    copy = pltpu.make_async_remote_copy(
                        src.at[layer, 0, :, columns(to, LANES)],
                        dst.at[layer, slot, pl.ds(dy * dec, dec)],
                        tok_s.at[layer, n, slot, dy],
                        tok_r.at[layer, n, slot, dy],
                        device_id={"seq": to},
                        device_id_type=MESH,
                    )
                    copy.start()
                    tok_copies.append(copy)
            if layer == 0 and slot == 1:
                for copy in w_copies:
                    copy.start()

    for copy in own_w:
        copy.start()

    final = enc_ref[...].astype(jnp.float32)
    inv[...] = lax.rsqrt(jnp.mean(final * final, axis=-1, keepdims=True) + 1e-6)
    normed[...] = final * inv[...]

    for copy in own_kv:
        copy.wait()
    for copy in kv_copies:
        copy.wait_recv()

    first_head = lax.broadcasted_iota(jnp.int32, (enc_all, LANES), 1) < HEAD_DIM
    exchanges = []
    for layer in range(layers):
        for src, dst in ((kb, km), (vb, vm)):
            rows = src[:, layer].astype(jnp.float32).reshape(enc_all, LANES)
            dst[pl.ds(0, enc_all), :] = jnp.where(first_head, rows, 0.0).astype(jnp.bfloat16)
            dst[pl.ds(enc_all, enc_all), :] = jnp.where(first_head, 0.0, rows).astype(jnp.bfloat16)
        acc_k[...] = jnp.zeros_like(acc_k)
        acc_v[...] = jnp.zeros_like(acc_v)

        def tokens(slot, carry, layer=layer):
            for n, dst in enumerate((qb, gb)):
                for dy in range(ROWS):
                    there = dst.at[layer, slot, pl.ds(dy * dec, dec)]
                    pltpu.make_async_copy(there, there, tok_r.at[layer, n, slot, dy]).wait()
            queries = qb[layer, slot]
            grads = gb[layer, slot]
            count = queries.shape[0]
            scores = lax.dot_general(
                km[...], queries, TRANSPOSED, preferred_element_type=jnp.float32
            ).reshape(2, enc_all, count)
            prob_grad = lax.dot_general(
                vm[...], grads, TRANSPOSED, preferred_element_type=jnp.float32
            ).reshape(2, enc_all, count)
            shifted = jnp.exp(scores - jnp.max(scores, axis=1, keepdims=True))
            probs = shifted * (1.0 / jnp.sum(shifted, axis=1, keepdims=True))
            delta = jnp.sum(probs * prob_grad, axis=1, keepdims=True)
            score_grad = (probs * (prob_grad - delta)).astype(jnp.bfloat16)
            acc_v[...] += jnp.dot(
                probs.astype(jnp.bfloat16).reshape(2 * enc_all, count),
                grads,
                preferred_element_type=jnp.float32,
            )
            acc_k[...] += jnp.dot(
                score_grad.reshape(2 * enc_all, count),
                queries,
                preferred_element_type=jnp.float32,
            )
            return carry

        lax.fori_loop(0, RING, tokens, 0)

        side = enc_all // ROWS
        for n, acc in enumerate((acc_k, acc_v)):
            grad = jnp.where(
                first_head, acc[pl.ds(0, enc_all), :], acc[pl.ds(enc_all, enc_all), :]
            ).astype(jnp.bfloat16)
            for row in range(ROWS):
                g_own[row, :, pl.ds((2 * layer + n) * LANES, LANES)] = grad[
                    row * side : (row + 1) * side
                ]
        block = pl.ds(2 * layer * LANES, 2 * LANES)
        exchange = pltpu.make_async_remote_copy(
            g_own.at[1 - y, :, block],
            g_far.at[:, block],
            x_s.at[layer],
            x_r.at[layer],
            device_id={"seq": across},
            device_id_type=MESH,
        )
        exchange.start()
        exchanges.append(exchange)

        if layer == 0:
            for copy in own_w:
                copy.wait()
            for copy in w_copies:
                copy.wait()
            there = w.at[:, columns(layers + core, 2 * LANES)]
            handed = pltpu.make_async_remote_copy(
                there,
                there,
                f_s,
                f_r,
                device_id={"dp": dp + 1 - 2 * core},
                device_id_type=MESH,
            )
            handed.start()

    own_depth = 2 * layers * LANES
    tile = min(512, quarter)

    def project(part_at, pieces, add):
        def one(index, carry):
            at = columns(part_at * (quarter // tile) + index, tile)
            terms = part[:, :, at].reshape(RING * enc, tile) if add else 0.0
            for grads, start, depth in pieces:
                terms = terms + lax.dot_general(
                    grads, w[at, pl.ds(start, depth)], TRANSPOSED, preferred_element_type=jnp.float32
                )
            part[:, :, at] = terms.reshape(RING, enc, tile)
            return carry

        lax.fori_loop(0, quarter // tile, one, 0)

    last_depth = 2 * LANES
    early_depth = own_depth - last_depth
    for exchange in exchanges[:-1]:
        exchange.wait_recv()
    handed.wait()
    early = (
        (g_own[y], 0, own_depth),
        (g_far[:, pl.ds(0, early_depth)], own_depth, early_depth),
    )
    for at in PARTS:
        project(at, early, False)
    exchanges[-1].wait_recv()
    late = ((g_far[:, pl.ds(early_depth, last_depth)], own_depth + early_depth, last_depth),)

    hops = {}

    def term(dx, at):
        return part[lax.rem(x + dx + RING, RING), :, pl.ds(at * quarter, quarter)]

    def hop(at, left, k):
        way = -1 if left else 1
        length = HOPS[at][left]
        slot = FIRST[at][left] + k
        total = term(way * (length - k), at)
        if k:
            hops[at, left, k - 1].wait_recv()
            total = total + c_recv[slot - 1].astype(jnp.float32)
        c_send[slot] = total.astype(jnp.bfloat16)
        copy = pltpu.make_async_remote_copy(
            c_send.at[slot],
            c_recv.at[slot],
            c_s.at[slot],
            c_r.at[slot],
            device_id={"seq": member(way, 0)},
            device_id_type=MESH,
        )
        copy.start()
        hops[at, left, k] = copy

    for at in PARTS:
        project(at, late, True)
        hop(at, 0, 0)
        hop(at, 1, 0)
    for copy in kv_copies + tok_copies + exchanges:
        copy.wait_send()
    for k in range(1, 4):
        for at in PARTS:
            for left in range(2):
                if k < HOPS[at][left]:
                    hop(at, left, k)

    a_copies = []
    for at in PARTS:
        state = term(0, at)
        for left in range(2):
            last = HOPS[at][left] - 1
            hops[at, left, last].wait_recv()
            state = state + c_recv[FIRST[at][left] + last].astype(jnp.float32)
        cols = pl.ds(at * quarter, quarter)
        final_state[:, cols] = state
        gains = jnp.sum(state * normed[:, cols], axis=0, keepdims=True)
        for s in range(quarter // piece):
            a_send[at * (quarter // piece) + s] = gains[:, s * piece : (s + 1) * piece]
    for j, (dx, dy) in enumerate(others):
        to = member(dx, dy)
        copy = pltpu.make_async_remote_copy(
            a_send.at[to],
            a_recv.at[j],
            a_s.at[j],
            a_r.at[j],
            device_id={"seq": to},
            device_id_type=MESH,
        )
        copy.start()
        a_copies.append(copy)

    state = final_state[...]
    scaled = gain_ref[...] * state
    mean = jnp.mean(scaled * normed[...], axis=-1, keepdims=True)
    out_ref[...] = (inv[...] * (scaled - normed[...] * mean)).astype(jnp.bfloat16)

    total = a_send[seq]
    for copy in a_copies:
        copy.wait_recv()
    for j in range(len(others)):
        total = total + a_recv[j]

    def everyone(total, send, recv, here, dps, ss, rs):
        send[...] = total
        recv[here] = total
        copies = []
        for j, other in enumerate(dps):
            copy = pltpu.make_async_remote_copy(
                send,
                recv.at[here],
                ss.at[j],
                rs.at[j],
                device_id={"dp": other},
                device_id_type=MESH,
            )
            copy.start()
            copies.append(copy)
        for copy in copies:
            copy.wait_recv()
        total = recv[0]
        for j in range(1, len(dps) + 1):
            total = total + recv[j]
        return total, copies

    total, b_copies = everyone(total, b_send, b_recv, low, low_dps, b_s, b_r)
    total, z_copies = everyone(total, z_send, z_recv, z, z_dps, z_s, z_r)

    t_recv[seq] = total * (1.0 / (low_count * z_count))
    t_copies = []
    for j, (dx, dy) in enumerate(others):
        copy = pltpu.make_async_remote_copy(
            t_recv.at[seq],
            t_recv.at[seq],
            t_s.at[j],
            t_r.at[j],
            device_id={"seq": member(dx, dy)},
            device_id_type=MESH,
        )
        copy.start()
        t_copies.append(copy)
    for copy in list(hops.values()) + a_copies + b_copies + z_copies:
        copy.wait_send()
    for copy in t_copies:
        copy.wait()
    for s in range(RING * ROWS):
        gout_ref[:, pl.ds(s * piece, piece)] = t_recv[s]


def hand_over(grads_in, gains_in, grads_out, gains_out, sems):
    copies = (
        pltpu.make_async_copy(grads_in, grads_out, sems.at[0]),
        pltpu.make_async_copy(gains_in, gains_out, sems.at[1]),
    )
    for copy in copies:
        copy.start()
    for copy in copies:
        copy.wait()


def body(low_count, z_count, enc_final, norm_gain, q, g, k, v, kw, vw):
    enc, width = enc_final.shape[1:]
    layers, _, dec, _ = q.shape
    group = RING * ROWS
    enc_all = enc * group
    quarter = width // 4
    piece = width // group
    bf, f32 = jnp.bfloat16, jnp.float32
    dma = pltpu.SemaphoreType.DMA
    vmem = pltpu.VMEM
    outs = pl.pallas_call(
        functools.partial(kernel, low_count, z_count),
        out_shape=(
            jax.ShapeDtypeStruct((enc, width), bf),
            jax.ShapeDtypeStruct((1, width), f32),
        ),
        in_specs=[pl.BlockSpec(memory_space=vmem)] * 2 + [pl.BlockSpec(memory_space=pl.ANY)] * 6,
        out_specs=(pl.BlockSpec(memory_space=vmem),) * 2,
        scratch_shapes=[
            vmem((layers, RING, ROWS * dec, LANES), bf),
            vmem((layers, RING, ROWS * dec, LANES), bf),
            vmem((group, layers, enc, LANES), bf),
            vmem((group, layers, enc, LANES), bf),
            vmem((2 * enc_all, LANES), bf),
            vmem((2 * enc_all, LANES), bf),
            vmem((2 * enc_all, LANES), f32),
            vmem((2 * enc_all, LANES), f32),
            vmem((width, 4 * layers * LANES), bf),
            vmem((ROWS, enc_all // ROWS, 2 * layers * LANES), bf),
            vmem((enc_all // ROWS, 2 * layers * LANES), bf),
            vmem((RING, enc, width), f32),
            vmem((enc, width), f32),
            vmem((enc, width), f32),
            vmem((enc, 1), f32),
            vmem((CHAIN_SLOTS, enc, quarter), bf),
            vmem((CHAIN_SLOTS, enc, quarter), bf),
            vmem((group, 1, piece), f32),
            vmem((group, 1, piece), f32),
            vmem((1, piece), f32),
            vmem((low_count, 1, piece), f32),
            vmem((1, piece), f32),
            vmem((z_count, 1, piece), f32),
            vmem((group, 1, piece), f32),
            dma((layers, 2, RING, ROWS)),
            dma((layers, 2, RING, ROWS)),
            dma((2, RING, ROWS)),
            dma((2, RING, ROWS)),
            dma((layers, 2)),
            dma((2,)),
            dma((2,)),
            dma(()),
            dma(()),
            dma((layers,)),
            dma((layers,)),
            dma((CHAIN_SLOTS,)),
            dma((CHAIN_SLOTS,)),
            dma((group,)),
            dma((group,)),
            dma((low_count,)),
            dma((low_count,)),
            dma((z_count,)),
            dma((z_count,)),
            dma((group,)),
            dma((group,)),
        ],
        compiler_params=pltpu.CompilerParams(
            collective_id=0, has_side_effects=True, vmem_limit_bytes=56 * 2**20
        ),
    )(enc_final[0], norm_gain[None], q, g, k, v, kw, vw)
    grads, gains = pl.pallas_call(
        hand_over,
        out_shape=tuple(jax.ShapeDtypeStruct(o.shape, o.dtype) for o in outs),
        in_specs=[pl.BlockSpec(memory_space=pl.ANY)] * 2,
        out_specs=(pl.BlockSpec(memory_space=pl.ANY),) * 2,
        scratch_shapes=[dma((2,))],
    )(*outs)
    return grads[None], gains[0]


def solution(mesh):
    count = mesh.shape["dp"]
    low_count = min(8, count)
    placed = (
        P("dp", "seq", None),
        P(),
        P(None, "dp", "seq", None),
        P(None, "dp", "seq", None),
        P(None, "dp", "seq", None),
        P(None, "dp", "seq", None),
        P(None, None, "seq"),
        P(None, None, "seq"),
    )
    return jax.shard_map(
        functools.partial(body, low_count, count // low_count),
        mesh=mesh,
        in_specs=placed,
        out_specs=(P("dp", "seq", None), P()),
        check_vma=False,
    )
```

```python
import functools

import jax
import jax.numpy as jnp
from jax import lax
from jax.experimental import pallas as pl
from jax.experimental.pallas import tpu as pltpu
from jax.sharding import PartitionSpec as P

MESH = pl.DeviceIdType.MESH
HEAD_DIM = 64
LANES = 128
RING = 8
ROWS = 2
SHIFTS = (0, 4, 3, 5, 2, 6, 1, 7)
PARTS = (0, 4, 1, 5, 2, 6, 3, 7)
HOPS = ((4, 3),) * 4 + ((3, 4),) * 4
FIRST = tuple(tuple(sum(h[0] + h[1] for h in HOPS[:p]) + d * HOPS[p][0] for d in (0, 1)) for p in range(len(HOPS)))
CHAIN_SLOTS = sum(h[0] + h[1] for h in HOPS)

TRANSPOSED = (((1,), (1,)), ((), ()))


def kernel(
    low_count, z_count,
    enc_ref, gain_ref, q_ref, g_ref, k_ref, v_ref, kw_ref, vw_ref,
    out_ref, gout_ref,
    qb, gb, kb, vb, km, vm, acc_k, acc_v, w, g_own, g_far, part, final_state, normed, inv,
    c_send, c_recv, a_send, a_recv, b_send, b_recv, z_send, z_recv, t_recv,
    tok_s, tok_r, kv_s, kv_r, own_s, w_s, w_r, f_s, f_r, x_s, x_r, c_s, c_r,
    a_s, a_r, b_s, b_r, z_s, z_r, t_s, t_r,
):
    layers = q_ref.shape[0]
    dec = q_ref.shape[2]
    enc = k_ref.shape[2]
    enc_all = enc * RING * ROWS
    width = enc_ref.shape[1]
    strip = width // len(PARTS)
    piece = width // (RING * ROWS)
    yh_count = low_count // 2

    seq = lax.axis_index("seq")
    dp = lax.axis_index("dp")
    x = lax.rem(seq, RING)
    y = seq // RING
    low = lax.rem(dp, low_count)
    z = dp // low_count
    core = lax.rem(low, 2)
    y_hi = low // 2

    def member(dx, dy):
        return lax.rem(y + dy, ROWS) * RING + lax.rem(x + dx + RING, RING)

    def columns(index, size):
        return pl.ds(pl.multiple_of(index * size, size), size)

    others = [(dx, dy) for dx in SHIFTS for dy in range(ROWS) if (dx, dy) != (0, 0)]
    across = member(0, 1)
    far_yh = lax.rem(y_hi + 2 * y - 1 + yh_count, yh_count)
    far_dp = z * low_count + far_yh * 2 + core
    low_dps = [z * low_count + lax.rem(low + j, low_count) for j in range(1, low_count)]
    z_dps = [lax.rem(z + j, z_count) * low_count + low for j in range(1, z_count)]

    barrier = pltpu.get_barrier_semaphore()
    for dx, dy in others:
        pl.semaphore_signal(
            barrier, inc=1, device_id={"seq": member(dx, dy)}, device_id_type=MESH
        )
    for other in low_dps + z_dps:
        pl.semaphore_signal(barrier, inc=1, device_id={"dp": other}, device_id_type=MESH)
    pl.semaphore_signal(
        barrier, inc=1, device_id={"dp": far_dp, "seq": across}, device_id_type=MESH
    )

    own = []
    for layer in range(layers):
        for n, (src, dst) in enumerate(((q_ref, qb), (g_ref, gb))):
            own.append(
                pltpu.make_async_copy(
                    src.at[layer, 0, :, columns(seq, LANES)],
                    dst.at[layer, 0, pl.ds(0, dec)],
                    tok_r.at[layer, n, 0, 0],
                )
            )
    own_kv = []
    for n, (src, dst) in enumerate(((k_ref, kb), (v_ref, vb))):
        own_kv.append(
            pltpu.make_async_copy(
                src.at[:, 0, :, columns(seq, LANES)], dst.at[seq], kv_r.at[n, 0, 0]
            )
        )
    own_w = []
    for layer in range(layers):
        for n, src in enumerate((kw_ref, vw_ref)):
            own_w.append(
                pltpu.make_async_copy(
                    src.at[layer],
                    w.at[:, pl.ds((2 * layer + n) * LANES, LANES)],
                    own_s.at[layer, n],
                )
            )
    for copy in own_kv + own:
        copy.start()

    pl.semaphore_wait(barrier, len(others) + len(low_dps) + len(z_dps) + 1)

    kv_copies = []
    for dx, dy in others:
        to = member(dx, dy)
        for n, (src, dst) in enumerate(((k_ref, kb), (v_ref, vb))):
            kv_copies.append(
                pltpu.make_async_remote_copy(
                    src.at[:, 0, :, columns(to, LANES)],
                    dst.at[seq],
                    kv_s.at[n, dx, dy],
                    kv_r.at[n, dx, dy],
                    device_id={"seq": to},
                    device_id_type=MESH,
                )
            )
    for copy in kv_copies:
        copy.start()

    w_dp = jnp.where(core == 0, dp, far_dp)
    w_copies = []
    for n, src in enumerate((kw_ref, vw_ref)):
        w_copies.append(
            pltpu.make_async_remote_copy(
                src.at[core],
                w.at[:, columns(2 * layers + 2 * core + n, LANES)],
                w_s.at[n],
                w_r.at[n],
                device_id={"dp": w_dp, "seq": across},
                device_id_type=MESH,
            )
        )

    tok_copies = []
    for layer in range(layers):
        for slot, dx in enumerate(SHIFTS):
            for dy in range(ROWS):
                if (dx, dy) == (0, 0):
                    continue
                to = member(dx, dy)
                for n, (src, dst) in enumerate(((q_ref, qb), (g_ref, gb))):
                    copy = pltpu.make_async_remote_copy(
                        src.at[layer, 0, :, columns(to, LANES)],
                        dst.at[layer, slot, pl.ds(dy * dec, dec)],
                        tok_s.at[layer, n, slot, dy],
                        tok_r.at[layer, n, slot, dy],
                        device_id={"seq": to},
                        device_id_type=MESH,
                    )
                    copy.start()
                    tok_copies.append(copy)
            if layer == 0 and slot == 1:
                for copy in w_copies:
                    copy.start()

    for copy in own_w:
        copy.start()

    final = enc_ref[...].astype(jnp.float32)
    inv[...] = lax.rsqrt(jnp.mean(final * final, axis=-1, keepdims=True) + 1e-6)
    normed[...] = final * inv[...]

    for copy in own_kv:
        copy.wait()
    for copy in kv_copies:
        copy.wait_recv()

    first_head = lax.broadcasted_iota(jnp.int32, (enc_all, LANES), 1) < HEAD_DIM
    exchanges = []
    for layer in range(layers):
        for src, dst in ((kb, km), (vb, vm)):
            rows = src[:, layer].astype(jnp.float32).reshape(enc_all, LANES)
            dst[pl.ds(0, enc_all), :] = jnp.where(first_head, rows, 0.0).astype(jnp.bfloat16)
            dst[pl.ds(enc_all, enc_all), :] = jnp.where(first_head, 0.0, rows).astype(jnp.bfloat16)
        acc_k[...] = jnp.zeros_like(acc_k)
        acc_v[...] = jnp.zeros_like(acc_v)

        def tokens(slot, carry, layer=layer):
            for n, dst in enumerate((qb, gb)):
                for dy in range(ROWS):
                    there = dst.at[layer, slot, pl.ds(dy * dec, dec)]
                    pltpu.make_async_copy(there, there, tok_r.at[layer, n, slot, dy]).wait()
            queries = qb[layer, slot]
            grads = gb[layer, slot]
            count = queries.shape[0]
            scores = lax.dot_general(
                km[...], queries, TRANSPOSED, preferred_element_type=jnp.float32
            ).reshape(2, enc_all, count)
            prob_grad = lax.dot_general(
                vm[...], grads, TRANSPOSED, preferred_element_type=jnp.float32
            ).reshape(2, enc_all, count)
            shifted = jnp.exp(scores - jnp.max(scores, axis=1, keepdims=True))
            probs = shifted * (1.0 / jnp.sum(shifted, axis=1, keepdims=True))
            delta = jnp.sum(probs * prob_grad, axis=1, keepdims=True)
            score_grad = (probs * (prob_grad - delta)).astype(jnp.bfloat16)
            acc_v[...] += jnp.dot(
                probs.astype(jnp.bfloat16).reshape(2 * enc_all, count),
                grads,
                preferred_element_type=jnp.float32,
            )
            acc_k[...] += jnp.dot(
                score_grad.reshape(2 * enc_all, count),
                queries,
                preferred_element_type=jnp.float32,
            )
            return carry

        lax.fori_loop(0, RING, tokens, 0)

        side = enc_all // ROWS
        for n, acc in enumerate((acc_k, acc_v)):
            grad = jnp.where(
                first_head, acc[pl.ds(0, enc_all), :], acc[pl.ds(enc_all, enc_all), :]
            ).astype(jnp.bfloat16)
            for row in range(ROWS):
                g_own[row, :, pl.ds((2 * layer + n) * LANES, LANES)] = grad[
                    row * side : (row + 1) * side
                ]
        block = pl.ds(2 * layer * LANES, 2 * LANES)
        exchange = pltpu.make_async_remote_copy(
            g_own.at[1 - y, :, block],
            g_far.at[:, block],
            x_s.at[layer],
            x_r.at[layer],
            device_id={"seq": across},
            device_id_type=MESH,
        )
        exchange.start()
        exchanges.append(exchange)

        if layer == 0:
            for copy in own_w:
                copy.wait()
            for copy in w_copies:
                copy.wait()
            there = w.at[:, columns(layers + core, 2 * LANES)]
            handed = pltpu.make_async_remote_copy(
                there,
                there,
                f_s,
                f_r,
                device_id={"dp": dp + 1 - 2 * core},
                device_id_type=MESH,
            )
            handed.start()

    own_depth = 2 * layers * LANES
    tile = min(512, strip)

    def project(part_at, pieces, add):
        def one(index, carry):
            at = columns(part_at * (strip // tile) + index, tile)
            terms = part[:, :, at].reshape(RING * enc, tile) if add else 0.0
            for grads, start, depth in pieces:
                terms = terms + lax.dot_general(
                    grads, w[at, pl.ds(start, depth)], TRANSPOSED, preferred_element_type=jnp.float32
                )
            part[:, :, at] = terms.reshape(RING, enc, tile)
            return carry

        lax.fori_loop(0, strip // tile, one, 0)

    last_depth = 2 * LANES
    early_depth = own_depth - last_depth
    for exchange in exchanges[:-1]:
        exchange.wait_recv()
    handed.wait()
    early = (
        (g_own[y], 0, own_depth),
        (g_far[:, pl.ds(0, early_depth)], own_depth, early_depth),
    )
    for at in PARTS:
        project(at, early, False)
    exchanges[-1].wait_recv()
    late = ((g_far[:, pl.ds(early_depth, last_depth)], own_depth + early_depth, last_depth),)

    hops = {}

    def term(dx, at):
        return part[lax.rem(x + dx + RING, RING), :, pl.ds(at * strip, strip)]

    def hop(at, left, k):
        way = -1 if left else 1
        length = HOPS[at][left]
        slot = FIRST[at][left] + k
        total = term(way * (length - k), at)
        if k:
            hops[at, left, k - 1].wait_recv()
            total = total + c_recv[slot - 1].astype(jnp.float32)
        c_send[slot] = total.astype(jnp.bfloat16)
        copy = pltpu.make_async_remote_copy(
            c_send.at[slot],
            c_recv.at[slot],
            c_s.at[slot],
            c_r.at[slot],
            device_id={"seq": member(way, 0)},
            device_id_type=MESH,
        )
        copy.start()
        hops[at, left, k] = copy

    for at in PARTS:
        project(at, late, True)
        hop(at, 0, 0)
        hop(at, 1, 0)
    for k in range(1, 4):
        for at in PARTS:
            for left in range(2):
                if k < HOPS[at][left]:
                    hop(at, left, k)

    a_copies = []
    for at in PARTS:
        state = term(0, at)
        for left in range(2):
            last = HOPS[at][left] - 1
            hops[at, left, last].wait_recv()
            state = state + c_recv[FIRST[at][left] + last].astype(jnp.float32)
        cols = pl.ds(at * strip, strip)
        final_state[:, cols] = state
        gains = jnp.sum(state * normed[:, cols], axis=0, keepdims=True)
        for s in range(strip // piece):
            a_send[at * (strip // piece) + s] = gains[:, s * piece : (s + 1) * piece]
    for j, (dx, dy) in enumerate(others):
        to = member(dx, dy)
        copy = pltpu.make_async_remote_copy(
            a_send.at[to],
            a_recv.at[j],
            a_s.at[j],
            a_r.at[j],
            device_id={"seq": to},
            device_id_type=MESH,
        )
        copy.start()
        a_copies.append(copy)

    state = final_state[...]
    scaled = gain_ref[...] * state
    mean = jnp.mean(scaled * normed[...], axis=-1, keepdims=True)
    out_ref[...] = (inv[...] * (scaled - normed[...] * mean)).astype(jnp.bfloat16)

    for copy in kv_copies + tok_copies + exchanges:
        copy.wait_send()

    total = a_send[seq]
    for copy in a_copies:
        copy.wait_recv()
    for j in range(len(others)):
        total = total + a_recv[j]

    def everyone(total, send, recv, here, dps, ss, rs):
        send[...] = total
        recv[here] = total
        copies = []
        for j, other in enumerate(dps):
            copy = pltpu.make_async_remote_copy(
                send,
                recv.at[here],
                ss.at[j],
                rs.at[j],
                device_id={"dp": other},
                device_id_type=MESH,
            )
            copy.start()
            copies.append(copy)
        for copy in copies:
            copy.wait_recv()
        total = recv[0]
        for j in range(1, len(dps) + 1):
            total = total + recv[j]
        return total, copies

    total, b_copies = everyone(total, b_send, b_recv, low, low_dps, b_s, b_r)
    total, z_copies = everyone(total, z_send, z_recv, z, z_dps, z_s, z_r)

    t_recv[seq] = total
    t_copies = []
    for j, (dx, dy) in enumerate(others):
        copy = pltpu.make_async_remote_copy(
            t_recv.at[seq],
            t_recv.at[seq],
            t_s.at[j],
            t_r.at[j],
            device_id={"seq": member(dx, dy)},
            device_id_type=MESH,
        )
        copy.start()
        t_copies.append(copy)
    for copy in list(hops.values()) + a_copies + b_copies + z_copies:
        copy.wait_send()
    for copy in t_copies:
        copy.wait()
    for s in range(RING * ROWS):
        gout_ref[:, pl.ds(s * piece, piece)] = t_recv[s]


def body(low_count, z_count, enc_final, norm_gain, q, g, k, v, kw, vw):
    enc, width = enc_final.shape[1:]
    layers, _, dec, _ = q.shape
    group = RING * ROWS
    enc_all = enc * group
    strip = width // len(PARTS)
    piece = width // group
    bf, f32 = jnp.bfloat16, jnp.float32
    dma = pltpu.SemaphoreType.DMA
    vmem = pltpu.VMEM
    outs = pl.pallas_call(
        functools.partial(kernel, low_count, z_count),
        out_shape=(
            jax.ShapeDtypeStruct((enc, width), bf),
            jax.ShapeDtypeStruct((1, width), f32),
        ),
        in_specs=[pl.BlockSpec(memory_space=vmem)] * 2 + [pl.BlockSpec(memory_space=pl.ANY)] * 6,
        out_specs=(pl.BlockSpec(memory_space=vmem),) * 2,
        scratch_shapes=[
            vmem((layers, RING, ROWS * dec, LANES), bf),
            vmem((layers, RING, ROWS * dec, LANES), bf),
            vmem((group, layers, enc, LANES), bf),
            vmem((group, layers, enc, LANES), bf),
            vmem((2 * enc_all, LANES), bf),
            vmem((2 * enc_all, LANES), bf),
            vmem((2 * enc_all, LANES), f32),
            vmem((2 * enc_all, LANES), f32),
            vmem((width, 4 * layers * LANES), bf),
            vmem((ROWS, enc_all // ROWS, 2 * layers * LANES), bf),
            vmem((enc_all // ROWS, 2 * layers * LANES), bf),
            vmem((RING, enc, width), f32),
            vmem((enc, width), f32),
            vmem((enc, width), f32),
            vmem((enc, 1), f32),
            vmem((CHAIN_SLOTS, enc, strip), bf),
            vmem((CHAIN_SLOTS, enc, strip), bf),
            vmem((group, 1, piece), f32),
            vmem((group, 1, piece), f32),
            vmem((1, piece), f32),
            vmem((low_count, 1, piece), f32),
            vmem((1, piece), f32),
            vmem((z_count, 1, piece), f32),
            vmem((group, 1, piece), f32),
            dma((layers, 2, RING, ROWS)),
            dma((layers, 2, RING, ROWS)),
            dma((2, RING, ROWS)),
            dma((2, RING, ROWS)),
            dma((layers, 2)),
            dma((2,)),
            dma((2,)),
            dma(()),
            dma(()),
            dma((layers,)),
            dma((layers,)),
            dma((CHAIN_SLOTS,)),
            dma((CHAIN_SLOTS,)),
            dma((group,)),
            dma((group,)),
            dma((low_count,)),
            dma((low_count,)),
            dma((z_count,)),
            dma((z_count,)),
            dma((group,)),
            dma((group,)),
        ],
        compiler_params=pltpu.CompilerParams(
            collective_id=0, has_side_effects=True, vmem_limit_bytes=56 * 2**20
        ),
    )(enc_final[0], norm_gain[None], q, g, k, v, kw, vw)
    grads, gains = outs
    return grads[None], gains[0] * (1.0 / (low_count * z_count))


def solution(mesh):
    count = mesh.shape["dp"]
    low_count = min(8, count)
    placed = (
        P("dp", "seq", None),
        P(),
        P(None, "dp", "seq", None),
        P(None, "dp", "seq", None),
        P(None, "dp", "seq", None),
        P(None, "dp", "seq", None),
        P(None, None, "seq"),
        P(None, None, "seq"),
    )
    return jax.shard_map(
        functools.partial(body, low_count, count // low_count),
        mesh=mesh,
        in_specs=placed,
        out_specs=(P("dp", "seq", None), P()),
        check_vma=False,
    )
```
